32 devices in a mesh: groups: 2 (over y), blk: 4 (over z), col: 2 (over x), rep: 2 (over core).
Axes of the slice: x: 2, y: 2, z: 4, core: 2. Of those that a mesh axis runs over, the one named last changes fastest.
Arguments:
- row_factors: bfloat16 [16384, 256], P(('groups', 'blk', 'rep')), parts along dimension 0, may hold values from -1.5 to 1.5
- col_factors: bfloat16 [4096, 256], P(('groups', 'blk', 'col')), parts along dimension 0, may hold values from -1.5 to 1.5
- counts: int32 [16384, 4, 512], P(('groups', 'blk', 'rep'), None, 'col'), parts along dimension 0, may hold values from 0 to 1024, as said below
- row_margin: int32 [16384], P(('groups', 'blk', 'rep')), parts along dimension 0, may hold values from 100 to 7996
- col_margin: int32 [4096], P('groups'), parts along dimension 0, may hold values from 10000 to 99999
Outputs:
- row_grad: float32 [16384, 256], P(('groups', 'blk', 'rep')), parts along dimension 0
- col_grad: float32 [4096, 256], P(('groups', 'blk', 'col')), parts along dimension 0
The draws below stay inside these ranges and needn't reach their ends.
There are 2 independent parts, one for each index of `groups`. The reference program is written for one: setup_inputs(seed, part) draws one part's arguments, and reference() takes and returns one part's arrays. A program takes and returns all parts, laid end to end along the dimension named above; each array names one. Nothing has to cross between parts.
Inputs may be any that keep to these rules, and one draw needn't show every extreme that they name: `counts`: zero marks pairs never seen together.
All inputs are finite; a program needn't handle non-finite values.
Results may differ from the reference program's by a relative error of at most 0.0027.
Values may be sent and summed in bfloat16 or wider, within the bound.
A program may use at most 64 MiB of HBM per device.

```python
import jax
import jax.numpy as jnp

K = 256
STEPS = 4
RBLK = 2048
CBW = 512
NROWS = 8192
NCOLS = 2048
N_BLK = 4


def draw_counts(key, part):
    key = jax.random.fold_in(key, 11)
    level_key, value_key, seen_key = jax.random.split(key, 3)
    full_shape = (NROWS, STEPS, CBW)
    levels = jax.random.randint(level_key, full_shape, 0, 11)
    ceiling = jnp.left_shift(jnp.ones(full_shape, jnp.int32), levels.astype(jnp.int32))
    drawn = 1 + jax.random.randint(value_key, full_shape, 0, 1024) % ceiling
    seen_mask = jax.random.randint(seen_key, full_shape, 0, 10) >= 3
    result = jnp.where(seen_mask, drawn, 0).astype(jnp.int32)
    return result.at[0, 0, 0].set(1024)


def draw_row_margin(key, part):
    key = jax.random.fold_in(key, 23)
    base_draw = jax.random.randint(key, (NROWS,), 100, 2000)
    ramp_factor = 1 + 4 * jnp.arange(NROWS, dtype=jnp.int32) // NROWS
    result = (base_draw * ramp_factor).astype(jnp.int32)
    return result.at[NROWS - 1].set(7996)


def place_ends(values, rng, low, high):
    shape = values.shape
    index_at = [jax.random.randint(jax.random.fold_in(rng, axis), (), 0, shape[axis]) for axis in range(len(shape))]
    values = values.at[tuple(index_at)].set(low)
    longest = shape.index(max(shape))
    index_at[longest] = (index_at[longest] + 1) % shape[longest]
    return values.at[tuple(index_at)].set(high)


def shard_levels(own_key, extent, cuts, least, top_value):
    gain = 1.0
    for dim, blocks in cuts:
        steps = jax.random.uniform(jax.random.fold_in(jax.random.fold_in(own_key, 6), dim), (blocks,), jnp.float32, least / len(cuts), top_value / len(cuts))
        gain = gain * jnp.repeat(jnp.exp(steps), extent[dim] // blocks).reshape((-1,) + (1,) * (len(extent) - 1 - dim))
    return gain


def noise(own_key, extent, scale, most, shards=(), kind=jnp.bfloat16):
    values = jax.random.normal(own_key, extent, jnp.float32) * scale
    if len(shards) > 0:
        values = shard_levels(own_key, extent, shards, -0.22, 0.18) * values
    return jnp.clip(values, min=-most, max=most).astype(kind)


def setup_inputs(seed: int = 0, part: int = 0) -> dict:
    splits = jax.random.split(jax.random.key(seed), 6)
    own_keys = jax.random.split(jax.random.fold_in(splits[5], part), 6)
    return {
        "row_factors": noise(own_keys[0], (NROWS, K), 0.25, 1.5, ((0, 8),)),
        "col_factors": noise(own_keys[1], (NCOLS, K), 0.25, 1.5, ((0, 8),)),
        "counts": draw_counts(jax.random.fold_in(jax.random.fold_in(splits[5], part), 71), part),
        "row_margin": draw_row_margin(jax.random.fold_in(jax.random.fold_in(splits[5], part), 71), part),
        "col_margin": place_ends(jax.random.randint(own_keys[4], (NCOLS,), 10000, 100000), jax.random.fold_in(own_keys[4], 1), 10000, 99999).astype(jnp.int32),
    }


def reference(row_factors, col_factors, counts, row_margin, col_margin):
    log_total = jnp.log(jnp.sum(row_margin.astype(jnp.float32)))
    row_base = log_total - jnp.log(row_margin.astype(jnp.float32))
    col_logs = jnp.log(col_margin.astype(jnp.float32))
    loss_scale = float(STEPS * CBW) ** (-0.5)
    half_steps = STEPS // 2
    row_grad = jnp.zeros((NROWS, K), jnp.float32)
    col_grad = jnp.zeros((NCOLS, K), jnp.float32)
    for shard_index in range(N_BLK):
        low = shard_index * RBLK
        shard_rows = row_factors[low:low + RBLK]
        for slot_index in range(STEPS):
            col_block = (shard_index + slot_index - half_steps) % N_BLK
            first_col = col_block * CBW
            block_factors = col_factors[first_col:first_col + CBW]
            tile_counts = counts[low:low + RBLK, slot_index, :]
            tile_score = jnp.dot(shard_rows, block_factors.T, preferred_element_type=jnp.float32)
            tile_base = row_base[low:low + RBLK][:, None] - col_logs[first_col:first_col + CBW][None, :]
            counted = tile_counts.astype(jnp.float32)
            target = jnp.log(jnp.maximum(counted, 1.0)) + tile_base
            confidence = 0.1 + 0.25 * jnp.sqrt(counted)
            tile_slope = jnp.where(tile_counts > 0, confidence * (tile_score - target), jax.nn.sigmoid(tile_score - tile_base))
            tile_slope = (tile_slope * loss_scale).astype(jnp.bfloat16)
            row_part = jnp.dot(tile_slope, block_factors, preferred_element_type=jnp.float32)
            col_part = jnp.dot(tile_slope.T, shard_rows, preferred_element_type=jnp.float32)
            row_grad = row_grad.at[low:low + RBLK].add(row_part)
            col_grad = col_grad.at[first_col:first_col + CBW].add(col_part)
    return (row_grad, col_grad)
```

```python
import functools

import jax
import jax.numpy as jnp
from jax import lax
from jax.experimental import pallas as pl
from jax.experimental.pallas import tpu as pltpu
from jax.sharding import PartitionSpec as P

MESH = pl.DeviceIdType.MESH
F32 = jnp.float32
BF16 = jnp.bfloat16
NT = (((1,), (1,)), ((), ()))
LANES = 128


def kernel(dims, rf_hbm, cf_hbm, cnt_hbm, rm_ref, cm_ref,
           parts, colout,
           rf, cfb, cnt, mar, rft, rb, ncl, racc, rbf, cacc, cin, csum, zout, zin, outv,
           cnt_sem, loc_sem, mar_s, mar_r, cf_s, cf_r, fw_s, fw_r,
           rep_s, rep_r, z_s, z_r, x_s, x_r, own_sem, fin_s, fin_r):
    blks, cols, slots, rchunk = dims
    rows, rank = rf.shape
    piece = cfb.shape[1]
    tiles = piece // LANES
    chunks = rows // rchunk
    half = slots // 2
    hp = piece // 2
    hk = rank // 2
    b = lax.axis_index("blk")
    c = lax.axis_index("col")
    r = lax.axis_index("rep")
    other = 1 - r
    loss_scale = float(slots * piece * cols) ** (-0.5)
    others = sorted([s for s in range(slots) if s != half], key=lambda s: abs(s - half))
    per_chunk = rchunk * tiles * slots

    bar = pltpu.get_barrier_semaphore()
    for d in range(blks):
        for e in range(2):
            if d or e:
                pl.semaphore_signal(bar, inc=1, device_id={"blk": lax.rem(b + d, blks), "rep": lax.rem(r + e, 2)},
                                    device_id_type=MESH)
    for k in range(1, cols):
        pl.semaphore_signal(bar, inc=1, device_id={"col": lax.rem(c + k, cols)}, device_id_type=MESH)

    rf_cp = pltpu.make_async_copy(rf_hbm, rf, loc_sem.at[0])
    rf_cp.start()
    cf_cp = pltpu.make_async_copy(cf_hbm, cfb.at[half], loc_sem.at[1])
    cf_cp.start()
    cnt_cp = []
    for i in range(chunks):
        at = pl.ds(i * per_chunk, per_chunk)
        cp = pltpu.make_async_copy(cnt_hbm.at[at], cnt.at[at], cnt_sem.at[i])
        cp.start()
        cnt_cp.append(cp)
    pl.semaphore_wait(bar, 2 * blks - 1 + cols - 1)

    sends = []
    mar_cp = []
    for d in range(blks):
        for e in range(2):
            if d or e:
                k = d * 2 + e
                cp = pltpu.make_async_remote_copy(
                    src_ref=rm_ref, dst_ref=mar.at[k], send_sem=mar_s.at[k], recv_sem=mar_r.at[k],
                    device_id={"blk": lax.rem(b + d, blks), "rep": lax.rem(r + e, 2)}, device_id_type=MESH)
                cp.start()
                mar_cp.append(cp)
    sends += mar_cp
    my_half = pl.ds(pl.multiple_of(r * hp, hp), hp)
    cf_in = {}
    for s in others:
        cp = pltpu.make_async_remote_copy(
            src_ref=cf_hbm.at[my_half], dst_ref=cfb.at[s, my_half], send_sem=cf_s.at[s], recv_sem=cf_r.at[s],
            device_id={"blk": lax.rem(b - s + half + blks, blks)}, device_id_type=MESH)
        cp.start()
        cf_in[s] = cp
    sends += list(cf_in.values())

    lrm = jnp.log(rm_ref[...].astype(F32))
    for g in range(rows // LANES):
        rb[pl.ds(g * LANES, LANES), :] = jnp.broadcast_to(lrm[g:g + 1, :], (LANES, LANES)).T
    rf_cp.wait()
    eye = (lax.broadcasted_iota(jnp.int32, (rank, rank), 0)
           == lax.broadcasted_iota(jnp.int32, (rank, rank), 1)).astype(F32).astype(BF16)
    for i in range(chunks):
        rft[i] = lax.dot_general(eye, rf[pl.ds(i * rchunk, rchunk), :], NT,
                                 preferred_element_type=F32).astype(BF16)
    msum = rm_ref[...].astype(F32)
    for cp, k in zip(mar_cp, range(1, 2 * blks)):
        cp.wait_recv()
        msum = msum + mar[k].astype(F32)
    total = jnp.sum(jnp.sum(msum, axis=0, keepdims=True), axis=1, keepdims=True)
    log_total = jnp.log(jnp.broadcast_to(total, (1, LANES)))
    for s in range(slots):
        block = lax.rem(b + s - half + blks, blks)
        for t in range(tiles):
            at = (block * cols + c) * tiles + t
            ncl[s, pl.ds(t, 1), :] = jnp.log(cm_ref[pl.ds(at, 1), :].astype(F32)) - log_total

    cf_cp.wait()
    for cp in cnt_cp:
        cp.wait()

    def tile_work(i, s, first_rows):
        at = pl.ds(pl.multiple_of(i * rchunk, rchunk), rchunk)
        score = lax.dot_general(rf[at, :], cfb[s], NT, preferred_element_type=F32)
        lr = rb[at, :]
        halves = []
        for t in range(tiles):
            n = cnt[pl.ds(i * per_chunk + t * slots + s, rchunk, stride=tiles * slots), :].astype(F32)
            x = score[:, t * LANES:(t + 1) * LANES] + (lr + ncl[s, pl.ds(t, 1), :])
            conf = 0.1 * loss_scale + (0.25 * loss_scale) * (n * lax.rsqrt(n))
            seen = conf * (x - jnp.log(n))
            unseen = (0.5 * loss_scale) * jnp.tanh(0.5 * x) + 0.5 * loss_scale
            halves.append(jnp.where(n > 0.0, seen, unseen).astype(BF16))
        slope = jnp.concatenate(halves, axis=1)
        row_part = jnp.dot(slope, cfb[s], preferred_element_type=F32)
        col_part = jnp.dot(rft[i], slope, preferred_element_type=F32)
        return row_part, col_part

    def add_col(i, s, col_part):
        @pl.when(i == 0)
        def _():
            cacc[s] = col_part

        @pl.when(i > 0)
        def _():
            cacc[s] += col_part

    give = pl.ds(pl.multiple_of(other * hk, hk), hk)
    keep = pl.ds(pl.multiple_of(r * hk, hk), hk)
    rep_cp = {}

    def start_rep(s):
        cp = pltpu.make_async_remote_copy(
            src_ref=cacc.at[s, give], dst_ref=cin.at[s], send_sem=rep_s.at[s], recv_sem=rep_r.at[s],
            device_id={"rep": other}, device_id_type=MESH)
        cp.start()
        rep_cp[s] = cp
        sends.append(cp)

    z_cp = {}

    def start_z(s):
        rep_cp[s].wait_recv()
        if s == half:
            csum[...] = cacc[s, keep, :] + cin[s]
            return
        zout[s] = (cacc[s, keep, :] + cin[s]).astype(BF16)
        cp = pltpu.make_async_remote_copy(
            src_ref=zout.at[s], dst_ref=zin.at[s], send_sem=z_s.at[s], recv_sem=z_r.at[s],
            device_id={"blk": lax.rem(b + s - half + blks, blks)}, device_id_type=MESH)
        cp.start()
        z_cp[s] = cp
        sends.append(cp)

    fw_cp = {}

    def forward(s):
        cf_in[s].wait_recv()
        cp = pltpu.make_async_remote_copy(
            src_ref=cfb.at[s, my_half], dst_ref=cfb.at[s, my_half], send_sem=fw_s.at[s], recv_sem=fw_r.at[s],
            device_id={"rep": other}, device_id_type=MESH)
        cp.start()
        fw_cp[s] = cp
        sends.append(cp)

    @pl.loop(0, chunks)
    def _(i):
        row_part, col_part = tile_work(i, half, True)
        racc[pl.ds(pl.multiple_of(i * rchunk, rchunk), rchunk), :] = row_part
        add_col(i, half, col_part)

    start_rep(half)
    for s in others:
        forward(s)
    for s in others:
        fw_cp[s].wait_recv()
    start_z(half)

    def x_copy(i, k):
        at = pl.ds(pl.multiple_of(i * rchunk, rchunk), rchunk)
        return pltpu.make_async_remote_copy(
            src_ref=rbf.at[at], dst_ref=parts.at[c, at], send_sem=x_s.at[k - 1, i], recv_sem=x_r.at[k - 1, i],
            device_id={"col": lax.rem(c + k, cols)}, device_id_type=MESH)

    def own_copy(i):
        at = pl.ds(pl.multiple_of(i * rchunk, rchunk), rchunk)
        return pltpu.make_async_copy(rbf.at[at], parts.at[c, at], own_sem.at[i])

    @pl.loop(0, chunks)
    def _(i):
        at = pl.ds(pl.multiple_of(i * rchunk, rchunk), rchunk)
        acc = racc[at, :]
        for s in others:
            row_part, col_part = tile_work(i, s, False)
            acc = acc + row_part
            add_col(i, s, col_part)
        rbf[at, :] = acc.astype(BF16)
        for k in range(1, cols):
            x_copy(i, k).start()
        own_copy(i).start()

    for s in others:
        start_rep(s)
    for s in others:
        start_z(s)
    acc = csum[...]
    for s in others:
        z_cp[s].wait_recv()
        acc = acc + zin[s].astype(F32)
    lane_half = pl.ds(pl.multiple_of(r * hk, hk), hk)
    outv[:, lane_half] = acc.T
    fin = pltpu.make_async_remote_copy(
        src_ref=outv.at[:, lane_half], dst_ref=outv.at[:, lane_half], send_sem=fin_s, recv_sem=fin_r,
        device_id={"rep": other}, device_id_type=MESH)
    fin.start()
    fin.wait_recv()
    out_cp = pltpu.make_async_copy(outv, colout, loc_sem.at[0])
    out_cp.start()
    for i in range(chunks):
        own_copy(i).wait()
        for k in range(1, cols):
            x_copy(i, k).wait()
    for cp in sends:
        cp.wait_send()
    fin.wait_send()
    out_cp.wait()


def per_device(blks, cols, row_factors, col_factors, counts, row_margin, col_margin):
    rows, rank = row_factors.shape
    piece = col_factors.shape[0]
    slots = counts.shape[1]
    tiles = piece // LANES
    rchunk = 256
    chunks = rows // rchunk
    flat = counts.reshape(rows, slots, tiles, LANES).transpose(0, 2, 1, 3).reshape(rows * tiles * slots, LANES)
    rm = row_margin.reshape(rows // LANES, LANES)
    cm = col_margin.reshape(-1, LANES)
    dma = pltpu.SemaphoreType.DMA
    vmem = pltpu.VMEM
    anyspec = pl.BlockSpec(memory_space=pl.ANY)
    vspec = pl.BlockSpec(memory_space=pltpu.VMEM)
    cells = rows * piece * slots
    parts, col_grad = pl.pallas_call(
        functools.partial(kernel, (blks, cols, slots, rchunk)),
        out_shape=(jax.ShapeDtypeStruct((cols, rows, rank), BF16),
                   jax.ShapeDtypeStruct((piece, rank), F32)),
        in_specs=[anyspec, anyspec, anyspec, vspec, vspec],
        out_specs=(anyspec, anyspec),
        scratch_shapes=[
            vmem((rows, rank), BF16),
            vmem((slots, piece, rank), BF16),
            vmem((rows * tiles * slots, LANES), jnp.int32),
            vmem((2 * blks, rows // LANES, LANES), jnp.int32),
            vmem((chunks, rank, rchunk), BF16),
            vmem((rows, LANES), F32),
            vmem((slots, tiles, LANES), F32),
            vmem((rows, rank), F32),
            vmem((rows, rank), BF16),
            vmem((slots, rank, piece), F32),
            vmem((slots, rank // 2, piece), F32),
            vmem((rank // 2, piece), F32),
            vmem((slots, rank // 2, piece), BF16),
            vmem((slots, rank // 2, piece), BF16),
            vmem((piece, rank), F32),
            dma((chunks,)), dma((2,)),
            dma((2 * blks,)), dma((2 * blks,)),
            dma((slots,)), dma((slots,)), dma((slots,)), dma((slots,)),
            dma((slots,)), dma((slots,)), dma((slots,)), dma((slots,)),
            dma((max(cols - 1, 1), chunks)), dma((max(cols - 1, 1), chunks)),
            dma((chunks,)), dma, dma,
        ],
        compiler_params=pltpu.CompilerParams(
            collective_id=0, has_side_effects=True, vmem_limit_bytes=44 * 1024 * 1024),
        cost_estimate=pl.CostEstimate(
            flops=6 * cells * rank, bytes_accessed=4 * cells, transcendentals=3 * cells),
    )(row_factors, col_factors, flat, rm, cm)
    return jnp.sum(parts.astype(F32), axis=0), col_grad


def solution(mesh):
    in_specs = (
        P(("groups", "blk", "rep"), None),
        P(("groups", "blk", "col"), None),
        P(("groups", "blk", "rep"), None, "col"),
        P(("groups", "blk", "rep")),
        P("groups"),
    )
    out_specs = (P(("groups", "blk", "rep"), None), P(("groups", "blk", "col"), None))
    body = functools.partial(per_device, mesh.shape["blk"], mesh.shape["col"])
    return jax.shard_map(body, mesh=mesh, in_specs=in_specs, out_specs=out_specs, check_vma=False)
```

```python
import functools

import jax
import jax.numpy as jnp
from jax import lax
from jax.experimental import pallas as pl
from jax.experimental.pallas import tpu as pltpu
from jax.sharding import PartitionSpec as P

MESH = pl.DeviceIdType.MESH
F32 = jnp.float32
BF16 = jnp.bfloat16
FIN = 60
NT = (((1,), (1,)), ((), ()))
LANES = 128


def kernel(dims, rf_hbm, cf_hbm, cnt_hbm, rm_hbm, cm_hbm,
           parts, colout,
           rf, cfb, cnt, rm_ref, cm_ref, mar, rft, rb, ncl, racc, rbf, cacc, cin, csum, zout, zin, outv,
           cnt_sem, loc_sem, mar_s, mar_r, cf_s, cf_r, fw_s, fw_r,
           rep_s, rep_r, z_s, z_r, x_s, x_r, own_sem, fin_s, fin_r):
    blks, cols, slots, rchunk = dims
    rows, rank = rf.shape
    piece = cfb.shape[1]
    tiles = piece // LANES
    chunks = rows // rchunk
    half = slots // 2
    hp = piece // 2
    hk = rank // 2
    b = lax.axis_index("blk")
    c = lax.axis_index("col")
    r = lax.axis_index("rep")
    other = 1 - r
    loss_scale = float(slots * piece * cols) ** (-0.5)
    near = jnp.where(b == 0, half + 1, half - 1)
    others = [near, 2 * half - near] + sorted(
        [s for s in range(slots) if abs(s - half) > 1], key=lambda s: abs(s - half))
    last = range(len(others))
    per_chunk = rchunk * tiles * slots

    bar = pltpu.get_barrier_semaphore()
    for d in range(blks):
        for e in range(2):
            if d or e:
                pl.semaphore_signal(bar, inc=1, device_id={"blk": lax.rem(b + d, blks), "rep": lax.rem(r + e, 2)},
                                    device_id_type=MESH)
    for k in range(1, cols):
        pl.semaphore_signal(bar, inc=1, device_id={"col": lax.rem(c + k, cols)}, device_id_type=MESH)

    rm_cp = pltpu.make_async_copy(rm_hbm, rm_ref, loc_sem.at[2])
    rm_cp.start()
    cm_cp = pltpu.make_async_copy(cm_hbm, cm_ref, loc_sem.at[3])
    cm_cp.start()
    rf_cp = pltpu.make_async_copy(rf_hbm, rf, loc_sem.at[0])
    rf_cp.start()
    cf_cp = pltpu.make_async_copy(cf_hbm, cfb.at[half], loc_sem.at[1])
    cf_cp.start()
    cnt_cp = []
    for i in range(chunks):
        at = pl.ds(i * per_chunk, per_chunk)
        cp = pltpu.make_async_copy(cnt_hbm.at[at], cnt.at[at], cnt_sem.at[i])
        cp.start()
        cnt_cp.append(cp)
    pl.semaphore_wait(bar, 2 * blks - 1 + cols - 1)

    sends = []
    mar_cp = []
    for d in range(blks):
        for e in range(2):
            if d or e:
                k = d * 2 + e
                cp = pltpu.make_async_remote_copy(
                    src_ref=rm_hbm, dst_ref=mar.at[k], send_sem=mar_s.at[k], recv_sem=mar_r.at[k],
                    device_id={"blk": lax.rem(b + d, blks), "rep": lax.rem(r + e, 2)}, device_id_type=MESH)
                cp.start()
                mar_cp.append(cp)
    sends += mar_cp
    my_half = pl.ds(pl.multiple_of(r * hp, hp), hp)
    cf_in = []
    for s in others:
        cp = pltpu.make_async_remote_copy(
            src_ref=cf_hbm.at[my_half], dst_ref=cfb.at[s, my_half], send_sem=cf_s.at[s], recv_sem=cf_r.at[s],
            device_id={"blk": lax.rem(b - s + half + blks, blks)}, device_id_type=MESH)
        cp.start()
        cf_in.append(cp)
    sends += cf_in

    rm_cp.wait()
    cm_cp.wait()
    lrm = jnp.log(rm_ref[...].astype(F32))
    for g in range(rows // LANES):
        rb[pl.ds(g * LANES, LANES), :] = jnp.broadcast_to(lrm[g:g + 1, :], (LANES, LANES)).T
    rf_cp.wait()
    eye = (lax.broadcasted_iota(jnp.int32, (rank, rank), 0)
           == lax.broadcasted_iota(jnp.int32, (rank, rank), 1)).astype(F32).astype(BF16)
    for i in range(chunks):
        rft[i] = lax.dot_general(eye, rf[pl.ds(i * rchunk, rchunk), :], NT,
                                 preferred_element_type=F32).astype(BF16)
    msum = rm_ref[...].astype(F32)
    for cp, k in zip(mar_cp, range(1, 2 * blks)):
        cp.wait_recv()
        msum = msum + mar[k].astype(F32)
    total = jnp.sum(jnp.sum(msum, axis=0, keepdims=True), axis=1, keepdims=True)
    log_total = jnp.log(jnp.broadcast_to(total, (1, LANES)))
    for s in range(slots):
        block = lax.rem(b + s - half + blks, blks)
        for t in range(tiles):
            at = (block * cols + c) * tiles + t
            ncl[s, pl.ds(t, 1), :] = jnp.log(cm_ref[pl.ds(at, 1), :].astype(F32)) - log_total

    cf_cp.wait()
    for cp in cnt_cp:
        cp.wait()

    def tile_work(i, s, first_rows):
        at = pl.ds(pl.multiple_of(i * rchunk, rchunk), rchunk)
        score = lax.dot_general(rf[at, :], cfb[s], NT, preferred_element_type=F32)
        lr = rb[at, :]
        halves = []
        for t in range(tiles):
            n = cnt[pl.ds(i * per_chunk + t * slots + s, rchunk, stride=tiles * slots), :].astype(F32)
            x = score[:, t * LANES:(t + 1) * LANES] + (lr + ncl[s, pl.ds(t, 1), :])
            conf = 0.1 * loss_scale + (0.25 * loss_scale) * (n * lax.rsqrt(n))
            seen = conf * (x - jnp.log(n))
            unseen = (0.5 * loss_scale) * jnp.tanh(0.5 * x) + 0.5 * loss_scale
            halves.append(jnp.where(n > 0.0, seen, unseen).astype(BF16))
        slope = jnp.concatenate(halves, axis=1)
        row_part = jnp.dot(slope, cfb[s], preferred_element_type=F32)
        col_part = jnp.dot(rft[i], slope, preferred_element_type=F32)
        return row_part, col_part

    def add_col(i, s, col_part):
        @pl.when(i == 0)
        def _():
            cacc[s] = col_part

        @pl.when(i > 0)
        def _():
            cacc[s] += col_part

    give = pl.ds(pl.multiple_of(other * hk, hk), hk)
    keep = pl.ds(pl.multiple_of(r * hk, hk), hk)

    def rep_copy(s):
        return pltpu.make_async_remote_copy(
            src_ref=cacc.at[s, give], dst_ref=cin.at[s], send_sem=rep_s.at[s], recv_sem=rep_r.at[s],
            device_id={"rep": other}, device_id_type=MESH)

    def start_rep(s):
        cp = rep_copy(s)
        cp.start()
        sends.append(cp)

    def z_copy(s):
        return pltpu.make_async_remote_copy(
            src_ref=zout.at[s], dst_ref=zin.at[s], send_sem=z_s.at[s], recv_sem=z_r.at[s],
            device_id={"blk": lax.rem(b + s - half + blks, blks)}, device_id_type=MESH)

    def start_z(s):
        rep_copy(s).wait_recv()
        zout[s] = (cacc[s, keep, :] + cin[s]).astype(BF16)
        cp = z_copy(s)
        cp.start()
        sends.append(cp)

    def fw_copy(s):
        return pltpu.make_async_remote_copy(
            src_ref=cfb.at[s, my_half], dst_ref=cfb.at[s, my_half], send_sem=fw_s.at[s], recv_sem=fw_r.at[s],
            device_id={"rep": other}, device_id_type=MESH)

    def forward(n):
        cf_in[n].wait_recv()
        cp = fw_copy(others[n])
        cp.start()
        sends.append(cp)

    def own_rows(i):
        row_part, col_part = tile_work(i, half, True)
        racc[pl.ds(pl.multiple_of(i * rchunk, rchunk), rchunk), :] = row_part
        add_col(i, half, col_part)

    def near_rows(i):
        row_part, col_part = tile_work(i, near, False)
        racc[pl.ds(pl.multiple_of(i * rchunk, rchunk), rchunk), :] += row_part
        add_col(i, near, col_part)

    pl.loop(0, chunks // 2)(own_rows)
    forward(0)
    pl.loop(chunks // 2, chunks)(own_rows)
    start_rep(half)
    forward(1)
    fw_copy(others[0]).wait_recv()
    pl.loop(0, chunks // 2)(near_rows)
    for n in last[2:]:
        forward(n)
    pl.loop(chunks // 2, chunks)(near_rows)
    start_rep(near)
    for n in last[1:]:
        fw_copy(others[n]).wait_recv()

    def x_copy(i, k):
        at = pl.ds(pl.multiple_of(i * rchunk, rchunk), rchunk)
        return pltpu.make_async_remote_copy(
            src_ref=rbf.at[at], dst_ref=parts.at[c, at], send_sem=x_s.at[k - 1, i], recv_sem=x_r.at[k - 1, i],
            device_id={"col": lax.rem(c + k, cols)}, device_id_type=MESH)

    def own_copy(i):
        at = pl.ds(pl.multiple_of(i * rchunk, rchunk), rchunk)
        return pltpu.make_async_copy(rbf.at[at], parts.at[c, at], own_sem.at[i])

    def rest_rows(i):
        at = pl.ds(pl.multiple_of(i * rchunk, rchunk), rchunk)
        acc = racc[at, :]
        for s in others[1:]:
            row_part, col_part = tile_work(i, s, False)
            acc = acc + row_part
            add_col(i, s, col_part)
        rbf[at, :] = acc.astype(BF16)
        for k in range(1, cols):
            x_copy(i, k).start()
        own_copy(i).start()

    pl.loop(0, 1)(rest_rows)
    start_z(near)
    pl.loop(1, chunks)(rest_rows)

    for s in others[1:]:
        start_rep(s)
    rep_copy(half).wait_recv()
    csum[...] = cacc[half, keep, :] + cin[half]
    for s in others[1:]:
        start_z(s)
    acc = csum[...]
    for s in others:
        z_copy(s).wait_recv()
        acc = acc + zin[s].astype(F32)
    lane_half = pl.ds(pl.multiple_of(r * hk, hk), hk)
    outv[:, lane_half] = acc.T
    fin = pltpu.make_async_remote_copy(
        src_ref=outv.at[:, lane_half], dst_ref=outv.at[:, lane_half], send_sem=fin_s, recv_sem=fin_r,
        device_id={"rep": other}, device_id_type=MESH)
    fin.start()
    fin.wait_recv()
    out_cp = pltpu.make_async_copy(outv, colout, loc_sem.at[0])
    out_cp.start()
    for i in range(chunks):
        own_copy(i).wait()
        for k in range(1, cols):
            x_copy(i, k).wait()
    for cp in sends:
        cp.wait_send()
    fin.wait_send()
    out_cp.wait()


def finish_kernel(parts, col, row_out, col_out, pin, vout, cv, in_sem, out_sem, col_sem):
    cols, rows = parts.shape[0], parts.shape[1]
    step = rows // 4
    col_in = pltpu.make_async_copy(col, cv, col_sem.at[0])
    col_cp = pltpu.make_async_copy(cv, col_out, col_sem.at[1])
    at = [pl.ds(i * step, step) for i in range(4)]
    ins = [pltpu.make_async_copy(parts.at[:, a], pin.at[:, a], in_sem.at[i]) for i, a in enumerate(at)]
    outs = [pltpu.make_async_copy(vout.at[a], row_out.at[a], out_sem.at[i]) for i, a in enumerate(at)]
    for cp in ins:
        cp.start()
    col_in.start()
    for i, a in enumerate(at):
        ins[i].wait()
        acc = pin[0, a].astype(F32)
        for k in range(1, cols):
            acc = acc + pin[k, a].astype(F32)
        vout[a] = acc
        outs[i].start()
    col_in.wait()
    col_cp.start()
    for cp in outs:
        cp.wait()
    col_cp.wait()


def finish(parts, col):
    dma = pltpu.SemaphoreType.DMA
    anyspec = pl.BlockSpec(memory_space=pl.ANY)
    hspec = pl.BlockSpec(memory_space=pltpu.HBM)
    return pl.pallas_call(
        finish_kernel,
        out_shape=(jax.ShapeDtypeStruct(parts.shape[1:], F32), jax.ShapeDtypeStruct(col.shape, F32)),
        in_specs=[anyspec, anyspec],
        out_specs=(hspec, hspec),
        scratch_shapes=[pltpu.VMEM(parts.shape, BF16), pltpu.VMEM(parts.shape[1:], F32),
                        pltpu.VMEM(col.shape, F32), dma((4,)), dma((4,)), dma((2,))],
        compiler_params=pltpu.CompilerParams(vmem_limit_bytes=FIN * 1024 * 1024),
    )(parts, col)


def per_device(blks, cols, row_factors, col_factors, counts, row_margin, col_margin):
    rows, rank = row_factors.shape
    piece = col_factors.shape[0]
    slots = counts.shape[1]
    tiles = piece // LANES
    rchunk = 256
    chunks = rows // rchunk
    flat = counts.reshape(rows, slots, tiles, LANES).transpose(0, 2, 1, 3).reshape(rows * tiles * slots, LANES)
    rm = row_margin.reshape(rows // LANES, LANES)
    cm = col_margin.reshape(-1, LANES)
    dma = pltpu.SemaphoreType.DMA
    vmem = pltpu.VMEM
    anyspec = pl.BlockSpec(memory_space=pl.ANY)
    hspec = pl.BlockSpec(memory_space=pltpu.HBM)
    cells = rows * piece * slots
    parts, col_grad = pl.pallas_call(
        functools.partial(kernel, (blks, cols, slots, rchunk)),
        out_shape=(jax.ShapeDtypeStruct((cols, rows, rank), BF16),
                   jax.ShapeDtypeStruct((piece, rank), F32)),
        in_specs=[hspec] * 5,
        out_specs=(anyspec, anyspec),
        scratch_shapes=[
            vmem((rows, rank), BF16),
            vmem((slots, piece, rank), BF16),
            vmem((rows * tiles * slots, LANES), jnp.int32),
            vmem(rm.shape, jnp.int32),
            vmem(cm.shape, jnp.int32),
            vmem((2 * blks, rows // LANES, LANES), jnp.int32),
            vmem((chunks, rank, rchunk), BF16),
            vmem((rows, LANES), F32),
            vmem((slots, tiles, LANES), F32),
            vmem((rows, rank), F32),
            vmem((rows, rank), BF16),
            vmem((slots, rank, piece), F32),
            vmem((slots, rank // 2, piece), F32),
            vmem((rank // 2, piece), F32),
            vmem((slots, rank // 2, piece), BF16),
            vmem((slots, rank // 2, piece), BF16),
            vmem((piece, rank), F32),
            dma((chunks,)), dma((4,)),
            dma((2 * blks,)), dma((2 * blks,)),
            dma((slots,)), dma((slots,)), dma((slots,)), dma((slots,)),
            dma((slots,)), dma((slots,)), dma((slots,)), dma((slots,)),
            dma((max(cols - 1, 1), chunks)), dma((max(cols - 1, 1), chunks)),
            dma((chunks,)), dma, dma,
        ],
        compiler_params=pltpu.CompilerParams(
            collective_id=0, has_side_effects=True, vmem_limit_bytes=62 * 1024 * 1024),
        cost_estimate=pl.CostEstimate(
            flops=6 * cells * rank, bytes_accessed=4 * cells, transcendentals=3 * cells),
    )(row_factors, col_factors, flat, rm, cm)
    return finish(parts, col_grad)


def solution(mesh):
    in_specs = (
        P(("groups", "blk", "rep"), None),
        P(("groups", "blk", "col"), None),
        P(("groups", "blk", "rep"), None, "col"),
        P(("groups", "blk", "rep")),
        P("groups"),
    )
    out_specs = (P(("groups", "blk", "rep"), None), P(("groups", "blk", "col"), None))
    body = functools.partial(per_device, mesh.shape["blk"], mesh.shape["col"])
    return jax.shard_map(body, mesh=mesh, in_specs=in_specs, out_specs=out_specs, check_vma=False)
```

```python
import functools

import jax
import jax.numpy as jnp
from jax import lax
from jax.experimental import pallas as pl
from jax.experimental.pallas import tpu as pltpu
from jax.sharding import PartitionSpec as P

MESH = pl.DeviceIdType.MESH
F32 = jnp.float32
BF16 = jnp.bfloat16
FIN = 60
NT = (((1,), (1,)), ((), ()))
LANES = 128


def kernel(dims, rf_hbm, cf_hbm, cnt_hbm, rm_hbm, cm_hbm,
           parts, colout,
           rf, cfb, cnt, rm_ref, cm_ref, msrc, mar, rft, rb, ncl, racc, rbf, cacc, cin, csum, zout, zin, outv,
           cnt_sem, loc_sem, mar_s, mar_r, cf_s, cf_r, fw_s, fw_r,
           rep_s, rep_r, z_s, z_r, x_s, x_r, own_sem, fin_s, fin_r):
    blks, cols, slots, rchunk = dims
    rows, rank = rf.shape
    piece = cfb.shape[1]
    tiles = piece // LANES
    chunks = rows // rchunk
    half = slots // 2
    hp = piece // 2
    hk = rank // 2
    b = lax.axis_index("blk")
    c = lax.axis_index("col")
    r = lax.axis_index("rep")
    other = 1 - r
    loss_scale = float(slots * piece * cols) ** (-0.5)
    near = jnp.where(b < blks // 2, half + 1, half - 1)
    others = [near, 2 * half - near] + sorted(
        [s for s in range(slots) if abs(s - half) > 1], key=lambda s: abs(s - half))
    last = range(len(others))
    per_chunk = rchunk * tiles * slots

    bar = pltpu.get_barrier_semaphore()
    for d in range(blks):
        for e in range(2):
            if d or e:
                pl.semaphore_signal(bar, inc=1, device_id={"blk": lax.rem(b + d, blks), "rep": lax.rem(r + e, 2)},
                                    device_id_type=MESH)
    for k in range(1, cols):
        pl.semaphore_signal(bar, inc=1, device_id={"col": lax.rem(c + k, cols)}, device_id_type=MESH)

    rm_cp = pltpu.make_async_copy(rm_hbm, rm_ref, loc_sem.at[2])
    rm_cp.start()
    cm_cp = pltpu.make_async_copy(cm_hbm, cm_ref, loc_sem.at[3])
    cm_cp.start()
    rf_cp = pltpu.make_async_copy(rf_hbm, rf, loc_sem.at[0])
    rf_cp.start()
    cf_cp = pltpu.make_async_copy(cf_hbm, cfb.at[half], loc_sem.at[1])
    cf_cp.start()
    cnt_cp = []
    for i in range(chunks):
        at = pl.ds(i * per_chunk, per_chunk)
        cp = pltpu.make_async_copy(cnt_hbm.at[at], cnt.at[at], cnt_sem.at[i])
        cp.start()
        cnt_cp.append(cp)
    rm_cp.wait()
    own_sum = jnp.sum(rm_ref[...].astype(F32), axis=0, keepdims=True)
    msrc[...] = own_sum
    pl.semaphore_wait(bar, 2 * blks - 1 + cols - 1)

    sends = []
    mar_cp = []
    for d in range(blks):
        for e in range(2):
            if d or e:
                k = d * 2 + e
                cp = pltpu.make_async_remote_copy(
                    src_ref=msrc, dst_ref=mar.at[k], send_sem=mar_s.at[k], recv_sem=mar_r.at[k],
                    device_id={"blk": lax.rem(b + d, blks), "rep": lax.rem(r + e, 2)}, device_id_type=MESH)
                cp.start()
                mar_cp.append(cp)
    sends += mar_cp
    my_half = pl.ds(pl.multiple_of(r * hp, hp), hp)
    cf_in = []
    for s in others[:1] + others[2:] + others[1:2]:
        cp = pltpu.make_async_remote_copy(
            src_ref=cf_hbm.at[my_half], dst_ref=cfb.at[s, my_half], send_sem=cf_s.at[s], recv_sem=cf_r.at[s],
            device_id={"blk": lax.rem(b - s + half + blks, blks)}, device_id_type=MESH)
        cp.start()
        cf_in.append(cp)
    cf_in = cf_in[:1] + cf_in[-1:] + cf_in[1:-1]
    sends += cf_in

    cm_cp.wait()
    lrm = jnp.log(rm_ref[...].astype(F32))
    for g in range(rows // LANES):
        rb[pl.ds(g * LANES, LANES), :] = jnp.broadcast_to(lrm[g:g + 1, :], (LANES, LANES)).T
    rf_cp.wait()
    eye = (lax.broadcasted_iota(jnp.int32, (rank, rank), 0)
           == lax.broadcasted_iota(jnp.int32, (rank, rank), 1)).astype(F32).astype(BF16)
    for i in range(chunks):
        rft[i] = lax.dot_general(eye, rf[pl.ds(i * rchunk, rchunk), :], NT,
                                 preferred_element_type=F32).astype(BF16)
    msum = own_sum
    for cp, k in zip(mar_cp, range(1, 2 * blks)):
        cp.wait_recv()
        msum = msum + mar[k]
    total = jnp.sum(msum, axis=1, keepdims=True)
    log_total = jnp.log(jnp.broadcast_to(total, (1, LANES)))
    for s in range(slots):
        block = lax.rem(b + s - half + blks, blks)
        for t in range(tiles):
            at = (block * cols + c) * tiles + t
            ncl[s, pl.ds(t, 1), :] = jnp.log(cm_ref[pl.ds(at, 1), :].astype(F32)) - log_total

    cf_cp.wait()
    for cp in cnt_cp:
        cp.wait()

    def tile_work(i, s, first_rows):
        at = pl.ds(pl.multiple_of(i * rchunk, rchunk), rchunk)
        score = lax.dot_general(rf[at, :], cfb[s], NT, preferred_element_type=F32)
        lr = rb[at, :]
        halves = []
        for t in range(tiles):
            n = cnt[pl.ds(i * per_chunk + t * slots + s, rchunk, stride=tiles * slots), :].astype(F32)
            x = score[:, t * LANES:(t + 1) * LANES] + (lr + ncl[s, pl.ds(t, 1), :])
            conf = 0.1 * loss_scale + (0.25 * loss_scale) * (n * lax.rsqrt(n))
            seen = conf * (x - jnp.log(n))
            unseen = (0.5 * loss_scale) * jnp.tanh(0.5 * x) + 0.5 * loss_scale
            halves.append(jnp.where(n > 0.0, seen, unseen).astype(BF16))
        slope = jnp.concatenate(halves, axis=1)
        row_part = jnp.dot(slope, cfb[s], preferred_element_type=F32)
        col_part = jnp.dot(rft[i], slope, preferred_element_type=F32)
        return row_part, col_part

    def add_col(i, s, col_part):
        @pl.when(i == 0)
        def _():
            cacc[s] = col_part

        @pl.when(i > 0)
        def _():
            cacc[s] += col_part

    give = pl.ds(pl.multiple_of(other * hk, hk), hk)
    keep = pl.ds(pl.multiple_of(r * hk, hk), hk)

    def rep_copy(s):
        return pltpu.make_async_remote_copy(
            src_ref=cacc.at[s, give], dst_ref=cin.at[s], send_sem=rep_s.at[s], recv_sem=rep_r.at[s],
            device_id={"rep": other}, device_id_type=MESH)

    def start_rep(s):
        cp = rep_copy(s)
        cp.start()
        sends.append(cp)

    def z_copy(s):
        return pltpu.make_async_remote_copy(
            src_ref=zout.at[s], dst_ref=zin.at[s], send_sem=z_s.at[s], recv_sem=z_r.at[s],
            device_id={"blk": lax.rem(b + s - half + blks, blks)}, device_id_type=MESH)

    def start_z(s):
        rep_copy(s).wait_recv()
        zout[s] = (cacc[s, keep, :] + cin[s]).astype(BF16)
        cp = z_copy(s)
        cp.start()
        sends.append(cp)

    def fw_copy(s):
        return pltpu.make_async_remote_copy(
            src_ref=cfb.at[s, my_half], dst_ref=cfb.at[s, my_half], send_sem=fw_s.at[s], recv_sem=fw_r.at[s],
            device_id={"rep": other}, device_id_type=MESH)

    def forward(n):
        cf_in[n].wait_recv()
        cp = fw_copy(others[n])
        cp.start()
        sends.append(cp)

    def own_rows(i):
        row_part, col_part = tile_work(i, half, True)
        racc[pl.ds(pl.multiple_of(i * rchunk, rchunk), rchunk), :] = row_part
        add_col(i, half, col_part)

    def near_rows(i):
        row_part, col_part = tile_work(i, near, False)
        racc[pl.ds(pl.multiple_of(i * rchunk, rchunk), rchunk), :] += row_part
        add_col(i, near, col_part)

    pl.loop(0, chunks // 2, unroll=True)(own_rows)
    forward(0)
    pl.loop(chunks // 2, chunks, unroll=True)(own_rows)
    start_rep(half)
    forward(1)
    fw_copy(others[0]).wait_recv()
    pl.loop(0, chunks // 2, unroll=True)(near_rows)
    for n in last[2:]:
        forward(n)
    pl.loop(chunks // 2, chunks, unroll=True)(near_rows)
    start_rep(near)
    for n in last[1:]:
        fw_copy(others[n]).wait_recv()

    def x_copy(i, k):
        at = pl.ds(pl.multiple_of(i * rchunk, rchunk), rchunk)
        return pltpu.make_async_remote_copy(
            src_ref=rbf.at[at], dst_ref=parts.at[c, at], send_sem=x_s.at[k - 1, i], recv_sem=x_r.at[k - 1, i],
            device_id={"col": lax.rem(c + k, cols)}, device_id_type=MESH)

    def own_copy(i):
        at = pl.ds(pl.multiple_of(i * rchunk, rchunk), rchunk)
        return pltpu.make_async_copy(rbf.at[at], parts.at[c, at], own_sem.at[i])

    def rest_rows(i):
        at = pl.ds(pl.multiple_of(i * rchunk, rchunk), rchunk)
        acc = racc[at, :]
        for s in others[1:]:
            row_part, col_part = tile_work(i, s, False)
            acc = acc + row_part
            add_col(i, s, col_part)
        rbf[at, :] = acc.astype(BF16)
        for k in range(1, cols):
            x_copy(i, k).start()
        own_copy(i).start()

    pl.loop(0, 1)(rest_rows)
    start_z(near)
    pl.loop(1, chunks)(rest_rows)

    for s in others[1:]:
        start_rep(s)
    rep_copy(half).wait_recv()
    csum[...] = cacc[half, keep, :] + cin[half]
    for s in others[1:]:
        start_z(s)
    acc = csum[...]
    for s in others:
        z_copy(s).wait_recv()
        acc = acc + zin[s].astype(F32)
    lane_half = pl.ds(pl.multiple_of(r * hk, hk), hk)
    outv[:, lane_half] = acc.T
    fin = pltpu.make_async_remote_copy(
        src_ref=outv.at[:, lane_half], dst_ref=outv.at[:, lane_half], send_sem=fin_s, recv_sem=fin_r,
        device_id={"rep": other}, device_id_type=MESH)
    fin.start()
    fin.wait_recv()
    out_cp = pltpu.make_async_copy(outv, colout, loc_sem.at[0])
    out_cp.start()
    for i in range(chunks):
        own_copy(i).wait()
        for k in range(1, cols):
            x_copy(i, k).wait()
    for cp in sends:
        cp.wait_send()
    fin.wait_send()
    out_cp.wait()


def finish_kernel(parts, col, row_out, col_out, pin, vout, cv, in_sem, out_sem, col_sem):
    cols, rows = parts.shape[0], parts.shape[1]
    step = rows // 4
    col_in = pltpu.make_async_copy(col, cv, col_sem.at[0])
    col_cp = pltpu.make_async_copy(cv, col_out, col_sem.at[1])
    at = [pl.ds(i * step, step) for i in range(4)]
    ins = [pltpu.make_async_copy(parts.at[:, a], pin.at[:, a], in_sem.at[i]) for i, a in enumerate(at)]
    outs = [pltpu.make_async_copy(vout.at[a], row_out.at[a], out_sem.at[i]) for i, a in enumerate(at)]
    for cp in ins:
        cp.start()
    col_in.start()
    for i, a in enumerate(at):
        ins[i].wait()
        acc = pin[0, a].astype(F32)
        for k in range(1, cols):
            acc = acc + pin[k, a].astype(F32)
        vout[a] = acc
        outs[i].start()
    col_in.wait()
    col_cp.start()
    for cp in outs:
        cp.wait()
    col_cp.wait()


def finish(parts, col):
    dma = pltpu.SemaphoreType.DMA
    anyspec = pl.BlockSpec(memory_space=pl.ANY)
    hspec = pl.BlockSpec(memory_space=pltpu.HBM)
    return pl.pallas_call(
        finish_kernel,
        out_shape=(jax.ShapeDtypeStruct(parts.shape[1:], F32), jax.ShapeDtypeStruct(col.shape, F32)),
        in_specs=[anyspec, anyspec],
        out_specs=(hspec, hspec),
        scratch_shapes=[pltpu.VMEM(parts.shape, BF16), pltpu.VMEM(parts.shape[1:], F32),
                        pltpu.VMEM(col.shape, F32), dma((4,)), dma((4,)), dma((2,))],
        compiler_params=pltpu.CompilerParams(vmem_limit_bytes=FIN * 1024 * 1024),
    )(parts, col)


def per_device(blks, cols, row_factors, col_factors, counts, row_margin, col_margin):
    rows, rank = row_factors.shape
    piece = col_factors.shape[0]
    slots = counts.shape[1]
    tiles = piece // LANES
    rchunk = 256
    chunks = rows // rchunk
    flat = counts.reshape(rows, slots, tiles, LANES).transpose(0, 2, 1, 3).reshape(rows * tiles * slots, LANES)
    rm = row_margin.reshape(rows // LANES, LANES)
    cm = col_margin.reshape(-1, LANES)
    dma = pltpu.SemaphoreType.DMA
    vmem = pltpu.VMEM
    anyspec = pl.BlockSpec(memory_space=pl.ANY)
    hspec = pl.BlockSpec(memory_space=pltpu.HBM)
    cells = rows * piece * slots
    parts, col_grad = pl.pallas_call(
        functools.partial(kernel, (blks, cols, slots, rchunk)),
        out_shape=(jax.ShapeDtypeStruct((cols, rows, rank), BF16),
                   jax.ShapeDtypeStruct((piece, rank), F32)),
        in_specs=[hspec] * 5,
        out_specs=(anyspec, anyspec),
        scratch_shapes=[
            vmem((rows, rank), BF16),
            vmem((slots, piece, rank), BF16),
            vmem((rows * tiles * slots, LANES), jnp.int32),
            vmem(rm.shape, jnp.int32),
            vmem(cm.shape, jnp.int32),
            vmem((1, LANES), F32),
            vmem((2 * blks, 1, LANES), F32),
            vmem((chunks, rank, rchunk), BF16),
            vmem((rows, LANES), F32),
            vmem((slots, tiles, LANES), F32),
            vmem((rows, rank), F32),
            vmem((rows, rank), BF16),
            vmem((slots, rank, piece), F32),
            vmem((slots, rank // 2, piece), F32),
            vmem((rank // 2, piece), F32),
            vmem((slots, rank // 2, piece), BF16),
            vmem((slots, rank // 2, piece), BF16),
            vmem((piece, rank), F32),
            dma((chunks,)), dma((4,)),
            dma((2 * blks,)), dma((2 * blks,)),
            dma((slots,)), dma((slots,)), dma((slots,)), dma((slots,)),
            dma((slots,)), dma((slots,)), dma((slots,)), dma((slots,)),
            dma((max(cols - 1, 1), chunks)), dma((max(cols - 1, 1), chunks)),
            dma((chunks,)), dma, dma,
        ],
        compiler_params=pltpu.CompilerParams(
            collective_id=0, has_side_effects=True, vmem_limit_bytes=62 * 1024 * 1024),
        cost_estimate=pl.CostEstimate(
            flops=6 * cells * rank, bytes_accessed=4 * cells, transcendentals=3 * cells),
    )(row_factors, col_factors, flat, rm, cm)
    return finish(parts, col_grad)


def solution(mesh):
    in_specs = (
        P(("groups", "blk", "rep"), None),
        P(("groups", "blk", "col"), None),
        P(("groups", "blk", "rep"), None, "col"),
        P(("groups", "blk", "rep")),
        P("groups"),
    )
    out_specs = (P(("groups", "blk", "rep"), None), P(("groups", "blk", "col"), None))
    body = functools.partial(per_device, mesh.shape["blk"], mesh.shape["col"])
    return jax.shard_map(body, mesh=mesh, in_specs=in_specs, out_specs=out_specs, check_vma=False)
```
